32 devices in a mesh: date: 8 (over z, x), col: 4 (over y, core).
Axes of the slice: x: 2, y: 2, z: 4, core: 2. Of those that a mesh axis runs over, the one named last changes fastest.
Arguments:
- slc: float32 [2, 8, 32, 2048], P(None, 'date', None, 'col'), may hold values from -80 to 80
- offsets: int32 [8, 4], replicated, may hold values from 0 to 6, as said below
Outputs:
- interferogram: float32 [2, 8, 4, 8, 128], P(None, 'date', None, None, 'col')
- coherence: float32 [8, 4, 8, 128], P('date', None, None, 'col')
The draws below stay inside these ranges and needn't reach their ends.
Inputs may be any that keep to these rules, and one draw needn't show every extreme that they name: Row d lists the offsets of the pairs whose reference date is d; 0 marks an empty slot, the nonzero entries of a row are distinct, and d plus each offset is at most 7. Date 0 has 4 pairs, one of offset 6.
All inputs are finite; a program needn't handle non-finite values.
Results may differ from the reference program's by a relative error of at most 0.0003.
Values sent between devices are 32-bit elements; how exact they have to be, the bound alone decides.
A program may use at most 64 MiB of HBM per device.

```python
import math
import jax
import jax.numpy as jnp
from jax import lax

SLOTS = 4
MAX_OFFSET = 6
DATES = 8
ROWS = 32
COLS = 2048


def draw_slc(key, part):
    subkeys = jax.random.split(key, 4)
    full_shape = (2, DATES, ROWS, COLS)
    common = jnp.clip(jax.random.normal(subkeys[0], (2, 1, ROWS, COLS), jnp.float32), -6.0, 6.0)
    noise = jnp.clip(jax.random.normal(subkeys[1], full_shape, jnp.float32), -6.0, 6.0)
    mixing = jnp.exp(jax.random.uniform(subkeys[2], (1, DATES, ROWS, COLS), jnp.float32, math.log(0.3), math.log(3.0)))
    amplitude = jnp.exp(jax.random.uniform(subkeys[3], (1, 1, ROWS, COLS), jnp.float32, math.log(0.3), math.log(3.0)))
    return (amplitude * (common + mixing * noise)).astype(jnp.float32)


def draw_offsets(key, part):
    subkeys = jax.random.split(key, 2)
    scores = jax.random.randint(subkeys[0], (DATES, MAX_OFFSET), 0, 1 << 20)
    scores = scores * MAX_OFFSET + jnp.arange(MAX_OFFSET, dtype=jnp.int32)[None, :]
    ranked = jnp.argsort(scores, axis=1)[:, :SLOTS]
    chosen = (ranked + 1).astype(jnp.int32)
    kept = jax.random.randint(subkeys[1], (DATES, SLOTS), 0, 4) > 0
    first_row = (MAX_OFFSET - jnp.arange(SLOTS, dtype=jnp.int32)).astype(jnp.int32)
    date_rows = jnp.arange(DATES, dtype=jnp.int32)[:, None]
    chosen = jnp.where(date_rows == 0, first_row[None, :], chosen)
    kept = kept | (date_rows == 0)
    kept = kept & (date_rows + chosen <= DATES - 1)
    return jnp.where(kept, chosen, 0).astype(jnp.int32)


def setup_inputs(seed: int = 0) -> dict:
    streams_of = jax.random.split(jax.random.key(seed), 3)
    slc = draw_slc(jax.random.fold_in(streams_of[2], 71), 0)
    offsets = draw_offsets(jax.random.fold_in(streams_of[2], 71), 0)
    return dict(slc=slc, offsets=offsets)


epsilon = 1e-06

def look_sums(master_real, master_imag, partner_real, partner_imag, live_mask):
    prod_real = master_real * partner_real + master_imag * partner_imag
    prod_imag = master_imag * partner_real - master_real * partner_imag
    power_master = master_real * master_real + master_imag * master_imag
    power_partner = partner_real * partner_real + partner_imag * partner_imag
    power_master = jnp.broadcast_to(power_master, prod_real.shape)
    stacked = jnp.stack([prod_real, prod_imag, power_master, power_partner])
    full_shape = stacked.shape
    blocks = stacked.reshape(full_shape[:-2] + (full_shape[-2] // 4, 4, full_shape[-1] // 16, 16))
    looked = lax.optimization_barrier(jnp.sum(blocks, axis=(-3, -1))) / 64.0
    return looked * live_mask

def coherence_of(padded):
    row_count = padded.shape[-2] - 2
    col_count = padded.shape[-1] - 2
    window_sum = padded[..., 0:row_count, 0:col_count]
    for down_step in range(3):
        for side_step in range(3):
            if down_step or side_step:
                window_sum = window_sum + padded[..., down_step:down_step + row_count, side_step:side_step + col_count]
    magnitude = jnp.sqrt(window_sum[0] * window_sum[0] + window_sum[1] * window_sum[1])
    return magnitude / (jnp.sqrt(window_sum[2] * window_sum[3]) + epsilon)

def reference(slc, offsets):
    date_count = slc.shape[1]

    def one_date(reference_date):
        date_offsets = offsets[reference_date]
        live_mask = (date_offsets > 0).astype(jnp.float32)
        partner_index = jnp.clip(reference_date + date_offsets, 0, date_count - 1).astype(jnp.int32)
        master = slc[:, reference_date]
        partner = jnp.take(slc, partner_index, axis=1)
        return look_sums(master[0], master[1], partner[0], partner[1], live_mask[:, None, None])
    looked = lax.map(one_date, jnp.arange(date_count, dtype=jnp.int32))
    looked = jnp.moveaxis(looked, 0, 1)
    padded = jnp.pad(looked, ((0, 0), (0, 0), (0, 0), (1, 1), (1, 1)))
    return (looked[0:2], coherence_of(padded))
```

```python
import functools

import jax
import jax.numpy as jnp
from jax import lax
from jax.experimental import pallas as pl
from jax.experimental.pallas import tpu as pltpu
from jax.sharding import PartitionSpec as P

EPSILON = 1e-06
MAX_OFFSET = 6
LOOK_ROWS = 4
LOOK_COLS = 16
TILE = 8
LANES = 128
MESH = pl.DeviceIdType.MESH


def drain(ref, sem):
    pltpu.make_async_copy(ref, ref, sem).wait()


def split_dot(values, pool):
    total = None
    for _ in range(3):
        part = values.astype(jnp.bfloat16)
        values = values - part.astype(jnp.float32)
        dot = jnp.dot(part, pool, preferred_element_type=jnp.float32)
        total = dot if total is None else total + dot
    return total


def kernel(dates, cols, slots, slc, offsets, ifg, coh, blocks, offs, outbox, landed, halo, sems):
    date, col = lax.axis_index("date"), lax.axis_index("col")
    chunks = blocks.shape[1]
    width = chunks * LANES
    halves = slc.shape[2] // chunks
    cells = slc.shape[2] * LANES // LOOK_COLS
    rt, half = date // halves, date % halves
    side = lax.rem(col + cols + 2 * half - 1, cols)

    offs_copy = pltpu.make_async_copy(offsets, offs, sems.at[4])
    offs_copy.start()

    def tile_of(peer):
        return slc.at[:, peer // halves, pl.ds((peer % halves) * chunks, chunks)]

    my_rows = pl.ds(pl.multiple_of(date * TILE, TILE), TILE)
    pltpu.make_async_copy(tile_of(date), blocks.at[:, :, my_rows], sems.at[1]).start()

    barrier = pltpu.get_barrier_semaphore()
    for step in range(1, dates):
        peer = lax.rem(date + step, dates)
        pl.semaphore_signal(barrier, inc=1, device_id=(peer, col), device_id_type=MESH)
    for step in (1, cols - 1):
        other = lax.rem(col + step, cols)
        pl.semaphore_signal(barrier, inc=1, device_id=(date, other), device_id_type=MESH)
    pl.semaphore_wait(barrier, dates + 1)

    for step in range(1, dates):
        peer = lax.rem(date + step, dates)
        pltpu.make_async_remote_copy(
            src_ref=tile_of(peer),
            dst_ref=blocks.at[:, :, my_rows],
            send_sem=sems.at[0],
            recv_sem=sems.at[1],
            device_id=(peer, col),
            device_id_type=MESH,
        ).start()

    looked_col = lax.broadcasted_iota(jnp.int32, (width, LANES), 0) // LOOK_COLS
    per_half = width // LOOK_COLS
    shown = lax.broadcasted_iota(jnp.int32, (width, LANES), 1) % per_half
    pool = jnp.where(looked_col == shown, 1.0 / (LOOK_ROWS * LOOK_COLS), 0.0).astype(jnp.bfloat16)
    lane = lax.broadcasted_iota(jnp.int32, (dates, LANES), 1)
    offs_copy.wait()
    lane_off = jnp.zeros((dates, LANES), jnp.int32)
    for slot in range(slots):
        mine = (lane // cells == slot) & ((lane % cells) // per_half == half)
        lane_off = jnp.where(mine, offs[:, slot : slot + 1], lane_off)
    chosen = [lane_off == o for o in range(1, MAX_OFFSET + 1)]

    drain(blocks, sems.at[1])

    look_count = TILE // LOOK_ROWS
    pieces = []
    for look in range(look_count):
        real_sums = [None] * MAX_OFFSET
        imag_sums = [None] * MAX_OFFSET
        power = None
        for row in range(look * LOOK_ROWS, (look + 1) * LOOK_ROWS):
            a0, a1 = [
                jnp.concatenate(
                    [
                        blocks[comp, chunk, pl.ds(row, dates, stride=TILE), :]
                        for chunk in range(chunks)
                    ],
                    axis=1,
                )
                for comp in range(2)
            ]
            squares = a0 * a0 + a1 * a1
            power = squares if power is None else power + squares
            for o in range(1, MAX_OFFSET + 1):
                b0 = pltpu.roll(a0, dates - o, 0)
                b1 = pltpu.roll(a1, dates - o, 0)
                real = a0 * b0 + a1 * b1
                imag = a1 * b0 - a0 * b1
                real_sums[o - 1] = real if real_sums[o - 1] is None else real_sums[o - 1] + real
                imag_sums[o - 1] = imag if imag_sums[o - 1] is None else imag_sums[o - 1] + imag
        pieces += real_sums + imag_sums + [power]
    pooled = split_dot(jnp.concatenate(pieces, axis=0), pool)

    count = 2 * MAX_OFFSET + 1
    for look in range(look_count):
        part = [
            pooled[(look * count + q) * dates : (look * count + q + 1) * dates] for q in range(count)
        ]
        planes = [jnp.zeros((dates, LANES), jnp.float32) for _ in range(4)]
        for o in range(1, MAX_OFFSET + 1):
            take = chosen[o - 1]
            planes[0] = jnp.where(take, part[o - 1], planes[0])
            planes[1] = jnp.where(take, part[MAX_OFFSET + o - 1], planes[1])
            planes[2] = jnp.where(take, part[2 * MAX_OFFSET], planes[2])
            planes[3] = jnp.where(take, pltpu.roll(part[2 * MAX_OFFSET], dates - o, 0), planes[3])
        for k in range(4):
            outbox[pl.ds(look * 4 + k, dates, stride=TILE), :] = planes[k]

    spot = pl.ds(pl.multiple_of(rt * TILE, TILE), TILE)
    for step in range(dates):
        peer = lax.rem(date + step, dates)
        tile = outbox.at[pl.ds(pl.multiple_of(peer * TILE, TILE), TILE)]
        if step:
            pltpu.make_async_remote_copy(
                src_ref=tile,
                dst_ref=landed.at[half, spot],
                send_sem=sems.at[2],
                recv_sem=sems.at[3],
                device_id=(peer, col),
                device_id_type=MESH,
            ).start()
        else:
            pltpu.make_async_copy(tile, landed.at[half, spot], sems.at[3]).start()
        pltpu.make_async_remote_copy(
            src_ref=tile,
            dst_ref=halo.at[half, spot],
            send_sem=sems.at[5],
            recv_sem=sems.at[6],
            device_id=(peer, side),
            device_id_type=MESH,
        ).start()

    look_rows = landed.shape[1] // 4
    lane = lax.broadcasted_iota(jnp.int32, (look_rows, LANES), 1) % cells
    line = lax.broadcasted_iota(jnp.int32, (look_rows, LANES), 0)
    left_edge, right_edge = lane == 0, lane == cells - 1
    has_left = jnp.where(col > 0, 1.0, 0.0)
    has_right = jnp.where(col < cols - 1, 1.0, 0.0)

    drain(landed, sems.at[3])
    drain(halo, sems.at[6])
    sums = []
    for k in range(4):
        plane = pl.ds(k, look_rows, stride=4)
        main = landed[0, plane, :]
        for other in range(1, halves):
            main = main + landed[other, plane, :]
        if k < 2:
            for slot in range(slots):
                ifg[k, 0, slot] = main[:, slot * cells : (slot + 1) * cells]
        after = pltpu.roll(halo[0, plane, :], cells - 1, 1) * has_right
        before = pltpu.roll(halo[halves - 1, plane, :], LANES - (cells - 1), 1) * has_left
        right = jnp.where(right_edge, after, pltpu.roll(main, LANES - 1, 1))
        left = jnp.where(left_edge, before, pltpu.roll(main, 1, 1))
        wide = main + left + right
        up = jnp.where(line == 0, 0.0, pltpu.roll(wide, 1, 0))
        down = jnp.where(line == look_rows - 1, 0.0, pltpu.roll(wide, look_rows - 1, 0))
        sums.append(wide + up + down)
    magnitude = jnp.sqrt(sums[0] * sums[0] + sums[1] * sums[1])
    result = magnitude / (jnp.sqrt(sums[2] * sums[3]) + EPSILON)
    for slot in range(slots):
        coh[0, slot] = result[:, slot * cells : (slot + 1) * cells]

    drain(blocks.at[:, :, pl.ds(0, (dates - 1) * TILE)], sems.at[0])
    drain(outbox.at[pl.ds(0, (dates - 1) * TILE)], sems.at[2])
    drain(outbox, sems.at[5])


def solution(mesh):
    dates, cols = mesh.shape["date"], mesh.shape["col"]

    def shards(slc, offsets):
        rows, columns = slc.shape[2], slc.shape[3]
        slots = offsets.shape[1]
        row_tiles = rows // TILE
        halves = dates // row_tiles
        if halves != 2 or slots * columns // LOOK_COLS != LANES:
            raise ValueError("unsupported sizes")
        width = columns // halves
        look_rows, cells = rows // LOOK_ROWS, columns // LOOK_COLS
        tiles = slc.reshape(2, row_tiles, TILE, columns // LANES, LANES).transpose(0, 1, 3, 2, 4)
        return tuple(
            pl.pallas_call(
                functools.partial(kernel, dates, cols, slots),
                out_shape=(
                    jax.ShapeDtypeStruct((2, 1, slots, look_rows, cells), jnp.float32),
                    jax.ShapeDtypeStruct((1, slots, look_rows, cells), jnp.float32),
                ),
                in_specs=[pl.BlockSpec(memory_space=pl.ANY)] * 2,
                out_specs=(pl.BlockSpec(memory_space=pltpu.VMEM),) * 2,
                scratch_shapes=[
                    pltpu.VMEM((2, width // LANES, dates * TILE, LANES), jnp.float32),
                    pltpu.VMEM(offsets.shape, jnp.int32),
                    pltpu.VMEM((dates * TILE, LANES), jnp.float32),
                    pltpu.VMEM((halves, row_tiles * TILE, LANES), jnp.float32),
                    pltpu.VMEM((halves, row_tiles * TILE, LANES), jnp.float32),
                    pltpu.SemaphoreType.DMA((7,)),
                ],
                compiler_params=pltpu.CompilerParams(
                    collective_id=0, has_side_effects=True, vmem_limit_bytes=16 * 1024 * 1024
                ),
            )(tiles, offsets)
        )

    return jax.shard_map(
        shards,
        mesh=mesh,
        in_specs=(P(None, "date", None, "col"), P()),
        out_specs=(P(None, "date", None, None, "col"), P("date", None, None, "col")),
        check_vma=False,
    )
```

```python
import functools

import jax
import jax.numpy as jnp
from jax import lax
from jax.experimental import pallas as pl
from jax.experimental.pallas import tpu as pltpu
from jax.sharding import PartitionSpec as P

EPSILON = 1e-06
MAX_OFFSET = 6
LOOK_ROWS = 4
LOOK_COLS = 16
TILE = 8
LANES = 128
MESH = pl.DeviceIdType.MESH


def drain(ref, sem):
    pltpu.make_async_copy(ref, ref, sem).wait()


def split_dot(values, pool):
    total = None
    for _ in range(3):
        part = values.astype(jnp.bfloat16)
        values = values - part.astype(jnp.float32)
        dot = jnp.dot(part, pool, preferred_element_type=jnp.float32)
        total = dot if total is None else total + dot
    return total


def kernel(dates, cols, slots, slc, offsets, dense, blocks, offs, outbox, landed, halo, sems):
    date, col = lax.axis_index("date"), lax.axis_index("col")
    chunks = blocks.shape[1]
    width = chunks * LANES
    halves = slc.shape[2] // chunks
    cells = slc.shape[2] * LANES // LOOK_COLS
    rt, half = date // halves, date % halves
    side = lax.rem(col + cols + 2 * half - 1, cols)

    order = sorted(range(1, dates), key=lambda step: abs(2 * step - dates))

    offs_copy = pltpu.make_async_copy(offsets, offs, sems.at[4])
    offs_copy.start()

    def tile_of(peer):
        return slc.at[:, peer // halves, pl.ds((peer % halves) * chunks, chunks)]

    my_rows = pl.ds(pl.multiple_of(date * TILE, TILE), TILE)
    pltpu.make_async_copy(tile_of(date), blocks.at[:, :, my_rows], sems.at[1]).start()

    barrier = pltpu.get_barrier_semaphore()
    for step in range(1, dates):
        peer = lax.rem(date + step, dates)
        pl.semaphore_signal(barrier, inc=1, device_id=(peer, col), device_id_type=MESH)
    for step in (1, cols - 1):
        other = lax.rem(col + step, cols)
        pl.semaphore_signal(barrier, inc=1, device_id=(date, other), device_id_type=MESH)
    pl.semaphore_wait(barrier, dates + 1)

    for step in order:
        peer = lax.rem(date + step, dates)
        pltpu.make_async_remote_copy(
            src_ref=tile_of(peer),
            dst_ref=blocks.at[:, :, my_rows],
            send_sem=sems.at[0],
            recv_sem=sems.at[1],
            device_id=(peer, col),
            device_id_type=MESH,
        ).start()

    looked_col = lax.broadcasted_iota(jnp.int32, (width, LANES), 0) // LOOK_COLS
    per_half = width // LOOK_COLS
    shown = lax.broadcasted_iota(jnp.int32, (width, LANES), 1) % per_half
    pool = jnp.where(looked_col == shown, 1.0 / (LOOK_ROWS * LOOK_COLS), 0.0).astype(jnp.bfloat16)
    lane = lax.broadcasted_iota(jnp.int32, (dates, LANES), 1)
    offs_copy.wait()
    lane_off = jnp.zeros((dates, LANES), jnp.int32)
    eye = lax.broadcasted_iota(jnp.int32, (dates, dates), 0) == lax.broadcasted_iota(
        jnp.int32, (dates, dates), 1
    )
    for slot in range(slots):
        row = offs[slot : slot + 1, :].astype(jnp.float32)
        column = jnp.sum(jnp.where(eye, row, 0.0), axis=1, keepdims=True).astype(jnp.int32)
        mine = (lane // cells == slot) & ((lane % cells) // per_half == half)
        lane_off = jnp.where(mine, column, lane_off)
    chosen = [lane_off == o for o in range(1, MAX_OFFSET + 1)]

    drain(blocks, sems.at[1])

    look_count = TILE // LOOK_ROWS
    pieces = []
    for look in range(look_count):
        real_sums = [None] * MAX_OFFSET
        imag_sums = [None] * MAX_OFFSET
        power = None
        for row in range(look * LOOK_ROWS, (look + 1) * LOOK_ROWS):
            a0, a1 = [
                jnp.concatenate(
                    [
                        blocks[comp, chunk, pl.ds(row, dates, stride=TILE), :]
                        for chunk in range(chunks)
                    ],
                    axis=1,
                )
                for comp in range(2)
            ]
            squares = a0 * a0 + a1 * a1
            power = squares if power is None else power + squares
            for o in range(1, MAX_OFFSET + 1):
                b0 = pltpu.roll(a0, dates - o, 0)
                b1 = pltpu.roll(a1, dates - o, 0)
                real = a0 * b0 + a1 * b1
                imag = a1 * b0 - a0 * b1
                real_sums[o - 1] = real if real_sums[o - 1] is None else real_sums[o - 1] + real
                imag_sums[o - 1] = imag if imag_sums[o - 1] is None else imag_sums[o - 1] + imag
        pieces += real_sums + imag_sums + [power]
    pooled = split_dot(jnp.concatenate(pieces, axis=0), pool)

    count = 2 * MAX_OFFSET + 1
    for look in range(look_count):
        part = [
            pooled[(look * count + q) * dates : (look * count + q + 1) * dates] for q in range(count)
        ]
        planes = [jnp.zeros((dates, LANES), jnp.float32) for _ in range(4)]
        for o in range(1, MAX_OFFSET + 1):
            take = chosen[o - 1]
            planes[0] = jnp.where(take, part[o - 1], planes[0])
            planes[1] = jnp.where(take, part[MAX_OFFSET + o - 1], planes[1])
            planes[2] = jnp.where(take, part[2 * MAX_OFFSET], planes[2])
            planes[3] = jnp.where(take, pltpu.roll(part[2 * MAX_OFFSET], dates - o, 0), planes[3])
        for k in range(4):
            outbox[pl.ds(look * 4 + k, dates, stride=TILE), :] = planes[k]

    spot = pl.ds(pl.multiple_of(rt * TILE, TILE), TILE)
    for step in order + [0]:
        peer = lax.rem(date + step, dates)
        tile = outbox.at[pl.ds(pl.multiple_of(peer * TILE, TILE), TILE)]
        if step:
            pltpu.make_async_remote_copy(
                src_ref=tile,
                dst_ref=landed.at[half, spot],
                send_sem=sems.at[2],
                recv_sem=sems.at[3],
                device_id=(peer, col),
                device_id_type=MESH,
            ).start()
        else:
            pltpu.make_async_copy(tile, landed.at[half, spot], sems.at[3]).start()
        pltpu.make_async_remote_copy(
            src_ref=tile,
            dst_ref=halo.at[half, spot],
            send_sem=sems.at[5],
            recv_sem=sems.at[6],
            device_id=(peer, side),
            device_id_type=MESH,
        ).start()

    look_rows = landed.shape[1] // 4
    lane = lax.broadcasted_iota(jnp.int32, (look_rows, LANES), 1) % cells
    line = lax.broadcasted_iota(jnp.int32, (look_rows, LANES), 0)
    left_edge, right_edge = lane == 0, lane == cells - 1
    has_left = jnp.where(col > 0, 1.0, 0.0)
    has_right = jnp.where(col < cols - 1, 1.0, 0.0)

    drain(landed, sems.at[3])
    drain(halo, sems.at[6])
    sums = []
    for k in range(4):
        plane = pl.ds(k, look_rows, stride=4)
        main = landed[0, plane, :]
        for other in range(1, halves):
            main = main + landed[other, plane, :]
        if k < 2:
            dense[k] = main
        after = pltpu.roll(halo[0, plane, :], cells - 1, 1) * has_right
        before = pltpu.roll(halo[halves - 1, plane, :], LANES - (cells - 1), 1) * has_left
        right = jnp.where(right_edge, after, pltpu.roll(main, LANES - 1, 1))
        left = jnp.where(left_edge, before, pltpu.roll(main, 1, 1))
        wide = main + left + right
        up = jnp.where(line == 0, 0.0, pltpu.roll(wide, 1, 0))
        down = jnp.where(line == look_rows - 1, 0.0, pltpu.roll(wide, look_rows - 1, 0))
        sums.append(wide + up + down)
    magnitude = jnp.sqrt(sums[0] * sums[0] + sums[1] * sums[1])
    dense[2] = magnitude / (jnp.sqrt(sums[2] * sums[3]) + EPSILON)

    drain(blocks.at[:, :, pl.ds(0, (dates - 1) * TILE)], sems.at[0])
    drain(outbox.at[pl.ds(0, (dates - 1) * TILE)], sems.at[2])
    drain(outbox, sems.at[5])


def spread(slots, dense, ifg, coh):
    cells = ifg.shape[-1]
    for slot in range(slots):
        part = slice(slot * cells, (slot + 1) * cells)
        ifg[0, 0, slot] = dense[0, :, part]
        ifg[1, 0, slot] = dense[1, :, part]
        coh[0, slot] = dense[2, :, part]


def solution(mesh):
    dates, cols = mesh.shape["date"], mesh.shape["col"]

    def shards(slc, offsets):
        rows, columns = slc.shape[2], slc.shape[3]
        slots = offsets.shape[1]
        row_tiles = rows // TILE
        halves = dates // row_tiles
        if halves != 2 or slots * columns // LOOK_COLS != LANES:
            raise ValueError("unsupported sizes")
        width = columns // halves
        look_rows, cells = rows // LOOK_ROWS, columns // LOOK_COLS
        tiles = slc.reshape(2, row_tiles, TILE, columns // LANES, LANES).transpose(0, 1, 3, 2, 4)
        dense = pl.pallas_call(
            functools.partial(kernel, dates, cols, slots),
            out_shape=jax.ShapeDtypeStruct((3, look_rows, LANES), jnp.float32),
            in_specs=[pl.BlockSpec(memory_space=pltpu.HBM)] * 2,
            out_specs=pl.BlockSpec(memory_space=pltpu.VMEM),
            scratch_shapes=[
                pltpu.VMEM((2, width // LANES, dates * TILE, LANES), jnp.float32),
                pltpu.VMEM((slots, dates), jnp.int32),
                pltpu.VMEM((dates * TILE, LANES), jnp.float32),
                pltpu.VMEM((halves, row_tiles * TILE, LANES), jnp.float32),
                pltpu.VMEM((halves, row_tiles * TILE, LANES), jnp.float32),
                pltpu.SemaphoreType.DMA((7,)),
            ],
            compiler_params=pltpu.CompilerParams(
                collective_id=0, has_side_effects=True, vmem_limit_bytes=55104 * 1024
            ),
        )(tiles, offsets.T)
        return tuple(
            pl.pallas_call(
                functools.partial(spread, slots),
                out_shape=(
                    jax.ShapeDtypeStruct((2, 1, slots, look_rows, cells), jnp.float32),
                    jax.ShapeDtypeStruct((1, slots, look_rows, cells), jnp.float32),
                ),
            )(dense)
        )

    return jax.shard_map(
        shards,
        mesh=mesh,
        in_specs=(P(None, "date", None, "col"), P()),
        out_specs=(P(None, "date", None, None, "col"), P("date", None, None, "col")),
        check_vma=False,
    )
```

```python
import functools

import jax
import jax.numpy as jnp
from jax import lax
from jax.experimental import pallas as pl
from jax.experimental.pallas import tpu as pltpu
from jax.sharding import PartitionSpec as P

EPSILON = 1e-06
MAX_OFFSET = 6
LOOK_ROWS = 4
LOOK_COLS = 16
TILE = 8
LANES = 128
MESH = pl.DeviceIdType.MESH


def drain(ref, sem):
    pltpu.make_async_copy(ref, ref, sem).wait()


def split_dot(values, pool):
    total = None
    for _ in range(3):
        part = values.astype(jnp.bfloat16)
        values = values - part.astype(jnp.float32)
        dot = jnp.dot(part, pool, preferred_element_type=jnp.float32)
        total = dot if total is None else total + dot
    return total


def kernel(dates, cols, slots, slc, offsets, dense, blocks, offs, outbox, landed, halo, sems):
    date, col = lax.axis_index("date"), lax.axis_index("col")
    chunks = blocks.shape[1]
    width = chunks * LANES
    halves = slc.shape[2] // chunks
    cells = slc.shape[2] * LANES // LOOK_COLS
    rt, half = date // halves, date % halves
    side = lax.rem(col + cols + 2 * half - 1, cols)

    order = sorted(range(1, dates), key=lambda step: abs(2 * step - dates))

    offs_copy = pltpu.make_async_copy(offsets, offs, sems.at[4])
    offs_copy.start()

    def tile_of(peer, chunk):
        return slc.at[:, peer // halves, (peer % halves) * chunks + chunk]

    my_rows = pl.ds(pl.multiple_of(date * TILE, TILE), TILE)
    for chunk in range(chunks):
        pltpu.make_async_copy(
            tile_of(date, chunk), blocks.at[:, chunk, my_rows], sems.at[6 + chunk]
        ).start()

    barrier = pltpu.get_barrier_semaphore()
    for step in range(1, dates):
        peer = lax.rem(date + step, dates)
        pl.semaphore_signal(barrier, inc=1, device_id=(peer, col), device_id_type=MESH)
    for step in (1, cols - 1):
        other = lax.rem(col + step, cols)
        pl.semaphore_signal(barrier, inc=1, device_id=(date, other), device_id_type=MESH)
    pl.semaphore_wait(barrier, dates + 1)

    for chunk in range(chunks):
        for step in order:
            peer = lax.rem(date + step, dates)
            pltpu.make_async_remote_copy(
                src_ref=tile_of(peer, chunk),
                dst_ref=blocks.at[:, chunk, my_rows],
                send_sem=sems.at[0],
                recv_sem=sems.at[6 + chunk],
                device_id=(peer, col),
                device_id_type=MESH,
            ).start()

    looked_col = lax.broadcasted_iota(jnp.int32, (width, LANES), 0) // LOOK_COLS
    per_half = width // LOOK_COLS
    shown = lax.broadcasted_iota(jnp.int32, (width, LANES), 1) % per_half
    pool = jnp.where(looked_col == shown, 1.0 / (LOOK_ROWS * LOOK_COLS), 0.0).astype(jnp.bfloat16)
    lane = lax.broadcasted_iota(jnp.int32, (dates, LANES), 1)
    offs_copy.wait()
    lane_off = jnp.zeros((dates, LANES), jnp.int32)
    eye = lax.broadcasted_iota(jnp.int32, (dates, dates), 0) == lax.broadcasted_iota(
        jnp.int32, (dates, dates), 1
    )
    for slot in range(slots):
        row = offs[slot : slot + 1, :].astype(jnp.float32)
        column = jnp.sum(jnp.where(eye, row, 0.0), axis=1, keepdims=True).astype(jnp.int32)
        mine = (lane // cells == slot) & ((lane % cells) // per_half == half)
        lane_off = jnp.where(mine, column, lane_off)
    chosen = [lane_off == o for o in range(1, MAX_OFFSET + 1)]

    look_count = TILE // LOOK_ROWS
    pooled = None
    for chunk in range(chunks):
        drain(blocks.at[:, chunk], sems.at[6 + chunk])
        pieces = []
        for look in range(look_count):
            real_sums = [None] * MAX_OFFSET
            imag_sums = [None] * MAX_OFFSET
            power = None
            for row in range(look * LOOK_ROWS, (look + 1) * LOOK_ROWS):
                a0 = blocks[0, chunk, pl.ds(row, dates, stride=TILE), :]
                a1 = blocks[1, chunk, pl.ds(row, dates, stride=TILE), :]
                squares = a0 * a0 + a1 * a1
                power = squares if power is None else power + squares
                for o in range(MAX_OFFSET):
                    b0 = pltpu.roll(a0, dates - 1 - o, 0)
                    b1 = pltpu.roll(a1, dates - 1 - o, 0)
                    real = a0 * b0 + a1 * b1
                    imag = a1 * b0 - a0 * b1
                    real_sums[o] = real if real_sums[o] is None else real_sums[o] + real
                    imag_sums[o] = imag if imag_sums[o] is None else imag_sums[o] + imag
            pieces += real_sums + imag_sums + [power]
        part = split_dot(
            jnp.concatenate(pieces, axis=0), pool[chunk * LANES : (chunk + 1) * LANES]
        )
        pooled = part if pooled is None else pooled + part

    count = 2 * MAX_OFFSET + 1
    for look in range(look_count):
        part = [
            pooled[(look * count + q) * dates : (look * count + q + 1) * dates] for q in range(count)
        ]
        planes = [jnp.zeros((dates, LANES), jnp.float32) for _ in range(4)]
        for o in range(1, MAX_OFFSET + 1):
            take = chosen[o - 1]
            planes[0] = jnp.where(take, part[o - 1], planes[0])
            planes[1] = jnp.where(take, part[MAX_OFFSET + o - 1], planes[1])
            planes[2] = jnp.where(take, part[2 * MAX_OFFSET], planes[2])
            planes[3] = jnp.where(take, pltpu.roll(part[2 * MAX_OFFSET], dates - o, 0), planes[3])
        for k in range(4):
            outbox[pl.ds(look * 4 + k, dates, stride=TILE), :] = planes[k]

    spot = pl.ds(pl.multiple_of(rt * TILE, TILE), TILE)
    for step in order + [0]:
        peer = lax.rem(date + step, dates)
        tile = outbox.at[pl.ds(pl.multiple_of(peer * TILE, TILE), TILE)]
        if step:
            pltpu.make_async_remote_copy(
                src_ref=tile,
                dst_ref=landed.at[half, spot],
                send_sem=sems.at[2],
                recv_sem=sems.at[3],
                device_id=(peer, col),
                device_id_type=MESH,
            ).start()
        else:
            pltpu.make_async_copy(tile, landed.at[half, spot], sems.at[3]).start()
        pltpu.make_async_remote_copy(
            src_ref=tile,
            dst_ref=halo.at[half, spot],
            send_sem=sems.at[5],
            recv_sem=sems.at[1],
            device_id=(peer, side),
            device_id_type=MESH,
        ).start()

    look_rows = landed.shape[1] // 4
    lane = lax.broadcasted_iota(jnp.int32, (look_rows, LANES), 1) % cells
    line = lax.broadcasted_iota(jnp.int32, (look_rows, LANES), 0)
    left_edge, right_edge = lane == 0, lane == cells - 1
    has_left = jnp.where(col > 0, 1.0, 0.0)
    has_right = jnp.where(col < cols - 1, 1.0, 0.0)

    drain(landed, sems.at[3])
    drain(halo, sems.at[1])
    sums = []
    for k in range(4):
        plane = pl.ds(k, look_rows, stride=4)
        main = landed[0, plane, :]
        for other in range(1, halves):
            main = main + landed[other, plane, :]
        if k < 2:
            dense[k] = main
        after = pltpu.roll(halo[0, plane, :], cells - 1, 1) * has_right
        before = pltpu.roll(halo[halves - 1, plane, :], LANES - (cells - 1), 1) * has_left
        right = jnp.where(right_edge, after, pltpu.roll(main, LANES - 1, 1))
        left = jnp.where(left_edge, before, pltpu.roll(main, 1, 1))
        wide = main + left + right
        up = jnp.where(line == 0, 0.0, pltpu.roll(wide, 1, 0))
        down = jnp.where(line == look_rows - 1, 0.0, pltpu.roll(wide, look_rows - 1, 0))
        sums.append(wide + up + down)
    magnitude = jnp.sqrt(sums[0] * sums[0] + sums[1] * sums[1])
    dense[2] = magnitude / (jnp.sqrt(sums[2] * sums[3]) + EPSILON)

    drain(blocks.at[:, :, pl.ds(0, (dates - 1) * TILE)], sems.at[0])
    drain(outbox.at[pl.ds(0, (dates - 1) * TILE)], sems.at[2])
    drain(outbox, sems.at[5])


def spread(slots, dense, ifg, coh):
    cells = ifg.shape[-1]
    for slot in range(slots):
        part = slice(slot * cells, (slot + 1) * cells)
        ifg[0, 0, slot] = dense[0, :, part]
        ifg[1, 0, slot] = dense[1, :, part]
        coh[0, slot] = dense[2, :, part]


def solution(mesh):
    dates, cols = mesh.shape["date"], mesh.shape["col"]

    def shards(slc, offsets):
        rows, columns = slc.shape[2], slc.shape[3]
        slots = offsets.shape[1]
        row_tiles = rows // TILE
        halves = dates // row_tiles
        if halves != 2 or slots * columns // LOOK_COLS != LANES:
            raise ValueError("unsupported sizes")
        width = columns // halves
        look_rows, cells = rows // LOOK_ROWS, columns // LOOK_COLS
        tiles = slc.reshape(2, row_tiles, TILE, columns // LANES, LANES).transpose(0, 1, 3, 2, 4)
        dense = pl.pallas_call(
            functools.partial(kernel, dates, cols, slots),
            out_shape=jax.ShapeDtypeStruct((3, look_rows, LANES), jnp.float32),
            in_specs=[pl.BlockSpec(memory_space=pltpu.HBM)] * 2,
            out_specs=pl.BlockSpec(memory_space=pltpu.VMEM),
            scratch_shapes=[
                pltpu.VMEM((2, width // LANES, dates * TILE, LANES), jnp.float32),
                pltpu.VMEM((slots, dates), jnp.int32),
                pltpu.VMEM((dates * TILE, LANES), jnp.float32),
                pltpu.VMEM((halves, row_tiles * TILE, LANES), jnp.float32),
                pltpu.VMEM((halves, row_tiles * TILE, LANES), jnp.float32),
                pltpu.SemaphoreType.DMA((6 + width // LANES,)),
            ],
            compiler_params=pltpu.CompilerParams(
                collective_id=0, has_side_effects=True, vmem_limit_bytes=8 * 1024 * 1024
            ),
        )(
            pltpu.with_memory_space_constraint(tiles, pltpu.HBM),
            pltpu.with_memory_space_constraint(offsets.T, pltpu.HBM),
        )
        return tuple(
            pl.pallas_call(
                functools.partial(spread, slots),
                out_shape=(
                    jax.ShapeDtypeStruct((2, 1, slots, look_rows, cells), jnp.float32),
                    jax.ShapeDtypeStruct((1, slots, look_rows, cells), jnp.float32),
                ),
                compiler_params=pltpu.CompilerParams(vmem_limit_bytes=1024 * 1024),
            )(dense)
        )

    return jax.shard_map(
        shards,
        mesh=mesh,
        in_specs=(P(None, "date", None, "col"), P()),
        out_specs=(P(None, "date", None, None, "col"), P("date", None, None, "col")),
        check_vma=False,
    )
```

```python
import functools

import jax
import jax.numpy as jnp
from jax import lax
from jax.experimental import pallas as pl
from jax.experimental.pallas import tpu as pltpu
from jax.sharding import PartitionSpec as P

EPSILON = 1e-06
MAX_OFFSET = 6
LOOK_ROWS = 4
LOOK_COLS = 16
TILE = 8
LANES = 128
MESH = pl.DeviceIdType.MESH


def drain(ref, sem):
    pltpu.make_async_copy(ref, ref, sem).wait()


def split_dot(values, pool):
    total = None
    for _ in range(3):
        part = values.astype(jnp.bfloat16)
        values = values - part.astype(jnp.float32)
        dot = jnp.dot(part, pool, preferred_element_type=jnp.float32)
        total = dot if total is None else total + dot
    return total


def kernel(dates, cols, slots, slc, offsets, dense, blocks, offs, outbox, landed, halo, unfolded, sems):
    date, col = lax.axis_index("date"), lax.axis_index("col")
    chunks = blocks.shape[1]
    width = chunks * LANES
    halves = slc.shape[2] // chunks
    cells = slc.shape[2] * LANES // LOOK_COLS
    rt, half = date // halves, date % halves
    side = lax.rem(col + cols + 2 * half - 1, cols)

    order = sorted(range(1, dates), key=lambda step: abs(2 * step - dates))

    offs_copy = pltpu.make_async_copy(offsets, offs, sems.at[4])
    offs_copy.start()

    def tile_of(peer):
        return slc.at[:, peer // halves, pl.ds((peer % halves) * chunks, chunks)]

    my_rows = pl.ds(pl.multiple_of(date * TILE, TILE), TILE)
    pltpu.make_async_copy(tile_of(date), blocks.at[:, :, my_rows], sems.at[6]).start()

    barrier = pltpu.get_barrier_semaphore()
    for step in range(1, dates):
        peer = lax.rem(date + step, dates)
        pl.semaphore_signal(barrier, inc=1, device_id=(peer, col), device_id_type=MESH)
    for step in (1, cols - 1):
        other = lax.rem(col + step, cols)
        pl.semaphore_signal(barrier, inc=1, device_id=(date, other), device_id_type=MESH)
    pl.semaphore_wait(barrier, dates + 1)

    for step in order:
        peer = lax.rem(date + step, dates)
        pltpu.make_async_remote_copy(
            src_ref=tile_of(peer),
            dst_ref=blocks.at[:, :, my_rows],
            send_sem=sems.at[0],
            recv_sem=sems.at[6],
            device_id=(peer, col),
            device_id_type=MESH,
        ).start()

    looked_col = lax.broadcasted_iota(jnp.int32, (width, LANES), 0) // LOOK_COLS
    per_half = width // LOOK_COLS
    shown = lax.broadcasted_iota(jnp.int32, (width, LANES), 1) % per_half
    pool = jnp.where(looked_col == shown, 1.0 / (LOOK_ROWS * LOOK_COLS), 0.0).astype(jnp.bfloat16)
    lane = lax.broadcasted_iota(jnp.int32, (dates, LANES), 1)
    offs_copy.wait()
    lane_off = jnp.zeros((dates, LANES), jnp.int32)
    eye = lax.broadcasted_iota(jnp.int32, (dates, dates), 0) == lax.broadcasted_iota(
        jnp.int32, (dates, dates), 1
    )
    for slot in range(slots):
        row = offs[slot : slot + 1, :].astype(jnp.float32)
        column = jnp.sum(jnp.where(eye, row, 0.0), axis=1, keepdims=True).astype(jnp.int32)
        mine = lane // cells == slot
        lane_off = jnp.where(mine, column, lane_off)
    chosen = [lane_off == o for o in range(1, MAX_OFFSET + 1)]

    look_count = TILE // LOOK_ROWS
    pooled = None
    drain(blocks, sems.at[6])
    for chunk in range(chunks):
        pieces = []
        for look in range(look_count):
            real_sums = [None] * MAX_OFFSET
            imag_sums = [None] * MAX_OFFSET
            power = None
            for row in range(look * LOOK_ROWS, (look + 1) * LOOK_ROWS):
                a0 = blocks[0, chunk, pl.ds(row, dates, stride=TILE), :]
                a1 = blocks[1, chunk, pl.ds(row, dates, stride=TILE), :]
                squares = a0 * a0 + a1 * a1
                power = squares if power is None else power + squares
                for o in range(MAX_OFFSET):
                    b0 = pltpu.roll(a0, dates - 1 - o, 0)
                    b1 = pltpu.roll(a1, dates - 1 - o, 0)
                    real = a0 * b0 + a1 * b1
                    imag = a1 * b0 - a0 * b1
                    real_sums[o] = real if real_sums[o] is None else real_sums[o] + real
                    imag_sums[o] = imag if imag_sums[o] is None else imag_sums[o] + imag
            pieces += real_sums + imag_sums + [power]
        part = split_dot(
            jnp.concatenate(pieces, axis=0), pool[chunk * LANES : (chunk + 1) * LANES]
        )
        pooled = part if pooled is None else pooled + part

    count = 2 * MAX_OFFSET + 1
    first = (lane % cells) // per_half == 0
    part = [
        jnp.where(
            first,
            pooled[q * dates : (q + 1) * dates],
            pooled[(count + q) * dates : (count + q + 1) * dates],
        )
        for q in range(count)
    ]
    planes = [jnp.zeros((dates, LANES), jnp.float32) for _ in range(4)]
    for o in range(1, MAX_OFFSET + 1):
        take = chosen[o - 1]
        planes[0] = jnp.where(take, part[o - 1], planes[0])
        planes[1] = jnp.where(take, part[MAX_OFFSET + o - 1], planes[1])
        planes[2] = jnp.where(take, part[2 * MAX_OFFSET], planes[2])
        planes[3] = jnp.where(take, pltpu.roll(part[2 * MAX_OFFSET], dates - o, 0), planes[3])
    for k in range(4):
        outbox[:, k, :] = planes[k]

    for step in order + [0]:
        peer = lax.rem(date + step, dates)
        tile = outbox.at[peer]
        if step:
            pltpu.make_async_remote_copy(
                src_ref=tile,
                dst_ref=landed.at[half, rt],
                send_sem=sems.at[2],
                recv_sem=sems.at[3],
                device_id=(peer, col),
                device_id_type=MESH,
            ).start()
        else:
            pltpu.make_async_copy(tile, landed.at[half, rt], sems.at[3]).start()
        pltpu.make_async_remote_copy(
            src_ref=tile,
            dst_ref=halo.at[half, rt],
            send_sem=sems.at[5],
            recv_sem=sems.at[1],
            device_id=(peer, side),
            device_id_type=MESH,
        ).start()

    row_tiles = landed.shape[1]
    look_rows = row_tiles * look_count
    lane = lax.broadcasted_iota(jnp.int32, (look_rows, LANES), 1) % cells
    line = lax.broadcasted_iota(jnp.int32, (look_rows, LANES), 0)
    left_edge, right_edge = lane == 0, lane == cells - 1
    has_left = jnp.where(col > 0, 1.0, 0.0)
    has_right = jnp.where(col < cols - 1, 1.0, 0.0)

    drain(landed, sems.at[3])
    drain(halo, sems.at[1])
    sums = []
    for k in range(4):
        ahead, behind = halo[0, :, k, :], halo[1, :, k, :]
        near, far = landed[0, :, k, :], landed[1, :, k, :]
        low = first[0:1]
        expanded = (
            (jnp.where(low, near, pltpu.roll(far, per_half, 1)), jnp.where(low, pltpu.roll(near, LANES - per_half, 1), far)),
            (pltpu.roll(ahead, cells - 1, 1), pltpu.roll(ahead, per_half - 1, 1)),
            (pltpu.roll(behind, LANES - per_half + 1, 1), pltpu.roll(behind, LANES - cells + 1, 1)),
        )
        for which in range(3):
            for look in range(look_count):
                unfolded[3 * k + which, pl.ds(look, row_tiles, stride=look_count), :] = expanded[which][look]
        main = unfolded[3 * k]
        if k < 2:
            dense[k] = main
        after = unfolded[3 * k + 1] * has_right
        before = unfolded[3 * k + 2] * has_left
        right = jnp.where(right_edge, after, pltpu.roll(main, LANES - 1, 1))
        left = jnp.where(left_edge, before, pltpu.roll(main, 1, 1))
        wide = main + left + right
        up = jnp.where(line == 0, 0.0, pltpu.roll(wide, 1, 0))
        down = jnp.where(line == look_rows - 1, 0.0, pltpu.roll(wide, look_rows - 1, 0))
        sums.append(wide + up + down)
    magnitude = jnp.sqrt(sums[0] * sums[0] + sums[1] * sums[1])
    dense[2] = magnitude / (jnp.sqrt(sums[2] * sums[3]) + EPSILON)

    drain(blocks.at[:, :, pl.ds(0, (dates - 1) * TILE)], sems.at[0])
    drain(outbox.at[pl.ds(0, dates - 1)], sems.at[2])
    drain(outbox, sems.at[5])


def spread(slots, dense, ifg, coh):
    cells = ifg.shape[-1]
    for slot in range(slots):
        part = slice(slot * cells, (slot + 1) * cells)
        ifg[0, 0, slot] = dense[0, :, part]
        ifg[1, 0, slot] = dense[1, :, part]
        coh[0, slot] = dense[2, :, part]


def solution(mesh):
    dates, cols = mesh.shape["date"], mesh.shape["col"]

    def shards(slc, offsets):
        rows, columns = slc.shape[2], slc.shape[3]
        slots = offsets.shape[1]
        row_tiles = rows // TILE
        halves = dates // row_tiles
        if halves != 2 or slots * columns // LOOK_COLS != LANES:
            raise ValueError("unsupported sizes")
        width = columns // halves
        look_rows, cells = rows // LOOK_ROWS, columns // LOOK_COLS
        tiles = slc.reshape(2, row_tiles, TILE, columns // LANES, LANES).transpose(0, 1, 3, 2, 4)
        dense = pl.pallas_call(
            functools.partial(kernel, dates, cols, slots),
            out_shape=jax.ShapeDtypeStruct((3, look_rows, LANES), jnp.float32),
            in_specs=[pl.BlockSpec(memory_space=pltpu.HBM)] * 2,
            out_specs=pl.BlockSpec(memory_space=pltpu.VMEM),
            scratch_shapes=[
                pltpu.VMEM((2, width // LANES, dates * TILE, LANES), jnp.float32),
                pltpu.VMEM((slots, dates), jnp.int32),
                pltpu.VMEM((dates, 4, LANES), jnp.float32),
                pltpu.VMEM((halves, row_tiles, 4, LANES), jnp.float32),
                pltpu.VMEM((halves, row_tiles, 4, LANES), jnp.float32),
                pltpu.VMEM((12, look_rows, LANES), jnp.float32),
                pltpu.SemaphoreType.DMA((7,)),
            ],
            compiler_params=pltpu.CompilerParams(
                collective_id=0, has_side_effects=True, vmem_limit_bytes=8 * 1024 * 1024
            ),
        )(
            pltpu.with_memory_space_constraint(tiles, pltpu.HBM),
            pltpu.with_memory_space_constraint(offsets.T, pltpu.HBM),
        )
        return tuple(
            pl.pallas_call(
                functools.partial(spread, slots),
                out_shape=(
                    jax.ShapeDtypeStruct((2, 1, slots, look_rows, cells), jnp.float32),
                    jax.ShapeDtypeStruct((1, slots, look_rows, cells), jnp.float32),
                ),
                compiler_params=pltpu.CompilerParams(vmem_limit_bytes=1024 * 1024),
            )(dense)
        )

    return jax.shard_map(
        shards,
        mesh=mesh,
        in_specs=(P(None, "date", None, "col"), P()),
        out_specs=(P(None, "date", None, None, "col"), P("date", None, None, "col")),
        check_vma=False,
    )
```

```python
import functools

import jax
import jax.numpy as jnp
from jax import lax
from jax.experimental import pallas as pl
from jax.experimental.pallas import tpu as pltpu
from jax.sharding import PartitionSpec as P

EPSILON = 1e-06
MAX_OFFSET = 6
LOOK_ROWS = 4
LOOK_COLS = 16
TILE = 8
LANES = 128
MESH = pl.DeviceIdType.MESH


def drain(ref, sem):
    pltpu.make_async_copy(ref, ref, sem).wait()


def split_dot(values, pool):
    total = None
    for _ in range(3):
        part = values.astype(jnp.bfloat16)
        values = values - part.astype(jnp.float32)
        dot = jnp.dot(part, pool, preferred_element_type=jnp.float32)
        total = dot if total is None else total + dot
    return total


def kernel(dates, cols, slots, slc, offsets, dense, blocks, offs, outbox, landed, halo, unfolded, staged, sems):
    date, col = lax.axis_index("date"), lax.axis_index("col")
    chunks = blocks.shape[1]
    width = chunks * LANES
    halves = slc.shape[2] // chunks
    cells = slc.shape[2] * LANES // LOOK_COLS
    rt, half = date // halves, date % halves
    side = lax.rem(col + cols + 2 * half - 1, cols)

    order = sorted(range(1, dates), key=lambda step: abs(2 * step - dates))

    offs_copy = pltpu.make_async_copy(offsets, offs, sems.at[4])
    offs_copy.start()

    stage_copy = pltpu.make_async_copy(slc, staged, sems.at[7])
    stage_copy.start()

    def tile_of(source, peer):
        return source.at[:, peer // halves, pl.ds((peer % halves) * chunks, chunks)]

    my_rows = pl.ds(pl.multiple_of(date * TILE, TILE), TILE)
    pltpu.make_async_copy(tile_of(slc, date), blocks.at[:, :, my_rows], sems.at[6]).start()

    barrier = pltpu.get_barrier_semaphore()
    for step in range(1, dates):
        peer = lax.rem(date + step, dates)
        pl.semaphore_signal(barrier, inc=1, device_id=(peer, col), device_id_type=MESH)
    for step in (1, cols - 1):
        other = lax.rem(col + step, cols)
        pl.semaphore_signal(barrier, inc=1, device_id=(date, other), device_id_type=MESH)
    pl.semaphore_wait(barrier, dates + 1)
    stage_copy.wait()

    for step in order:
        peer = lax.rem(date + step, dates)
        pltpu.make_async_remote_copy(
            src_ref=tile_of(staged, peer),
            dst_ref=blocks.at[:, :, my_rows],
            send_sem=sems.at[0],
            recv_sem=sems.at[6],
            device_id=(peer, col),
            device_id_type=MESH,
        ).start()

    looked_col = lax.broadcasted_iota(jnp.int32, (width, LANES), 0) // LOOK_COLS
    per_half = width // LOOK_COLS
    shown = lax.broadcasted_iota(jnp.int32, (width, LANES), 1) % per_half
    pool = jnp.where(looked_col == shown, 1.0 / (LOOK_ROWS * LOOK_COLS), 0.0).astype(jnp.bfloat16)
    lane = lax.broadcasted_iota(jnp.int32, (dates, LANES), 1)
    offs_copy.wait()
    lane_off = jnp.zeros((dates, LANES), jnp.int32)
    eye = lax.broadcasted_iota(jnp.int32, (dates, dates), 0) == lax.broadcasted_iota(
        jnp.int32, (dates, dates), 1
    )
    for slot in range(slots):
        row = offs[slot : slot + 1, :].astype(jnp.float32)
        column = jnp.sum(jnp.where(eye, row, 0.0), axis=1, keepdims=True).astype(jnp.int32)
        mine = lane // cells == slot
        lane_off = jnp.where(mine, column, lane_off)
    chosen = [lane_off == o for o in range(1, MAX_OFFSET + 1)]

    look_count = TILE // LOOK_ROWS
    pooled = None
    drain(blocks, sems.at[6])
    for chunk in range(chunks):
        pieces = []
        for look in range(look_count):
            real_sums = [None] * MAX_OFFSET
            imag_sums = [None] * MAX_OFFSET
            power = None
            for row in range(look * LOOK_ROWS, (look + 1) * LOOK_ROWS):
                a0 = blocks[0, chunk, pl.ds(row, dates, stride=TILE), :]
                a1 = blocks[1, chunk, pl.ds(row, dates, stride=TILE), :]
                squares = a0 * a0 + a1 * a1
                power = squares if power is None else power + squares
                for o in range(MAX_OFFSET):
                    b0 = pltpu.roll(a0, dates - 1 - o, 0)
                    b1 = pltpu.roll(a1, dates - 1 - o, 0)
                    real = a0 * b0 + a1 * b1
                    imag = a1 * b0 - a0 * b1
                    real_sums[o] = real if real_sums[o] is None else real_sums[o] + real
                    imag_sums[o] = imag if imag_sums[o] is None else imag_sums[o] + imag
            pieces += real_sums + imag_sums + [power]
        part = split_dot(
            jnp.concatenate(pieces, axis=0), pool[chunk * LANES : (chunk + 1) * LANES]
        )
        pooled = part if pooled is None else pooled + part

    count = 2 * MAX_OFFSET + 1
    first = (lane % cells) // per_half == 0
    part = [
        jnp.where(
            first,
            pooled[q * dates : (q + 1) * dates],
            pooled[(count + q) * dates : (count + q + 1) * dates],
        )
        for q in range(count)
    ]
    planes = [jnp.zeros((dates, LANES), jnp.float32) for _ in range(4)]
    for o in range(1, MAX_OFFSET + 1):
        take = chosen[o - 1]
        planes[0] = jnp.where(take, part[o - 1], planes[0])
        planes[1] = jnp.where(take, part[MAX_OFFSET + o - 1], planes[1])
        planes[2] = jnp.where(take, part[2 * MAX_OFFSET], planes[2])
        planes[3] = jnp.where(take, pltpu.roll(part[2 * MAX_OFFSET], dates - o, 0), planes[3])
    for k in range(4):
        outbox[:, k, :] = planes[k]

    for step in order + [0]:
        peer = lax.rem(date + step, dates)
        tile = outbox.at[peer]
        if step:
            pltpu.make_async_remote_copy(
                src_ref=tile,
                dst_ref=landed.at[half, rt],
                send_sem=sems.at[2],
                recv_sem=sems.at[3],
                device_id=(peer, col),
                device_id_type=MESH,
            ).start()
        else:
            pltpu.make_async_copy(tile, landed.at[half, rt], sems.at[3]).start()
        pltpu.make_async_remote_copy(
            src_ref=tile,
            dst_ref=halo.at[half, rt],
            send_sem=sems.at[5],
            recv_sem=sems.at[1],
            device_id=(peer, side),
            device_id_type=MESH,
        ).start()

    row_tiles = landed.shape[1]
    look_rows = row_tiles * look_count
    lane = lax.broadcasted_iota(jnp.int32, (look_rows, LANES), 1) % cells
    line = lax.broadcasted_iota(jnp.int32, (look_rows, LANES), 0)
    left_edge, right_edge = lane == 0, lane == cells - 1
    has_left = jnp.where(col > 0, 1.0, 0.0)
    has_right = jnp.where(col < cols - 1, 1.0, 0.0)

    drain(landed, sems.at[3])
    drain(halo, sems.at[1])
    sums = []
    for k in range(4):
        ahead, behind = halo[0, :, k, :], halo[1, :, k, :]
        near, far = landed[0, :, k, :], landed[1, :, k, :]
        low = first[0:1]
        expanded = (
            (jnp.where(low, near, pltpu.roll(far, per_half, 1)), jnp.where(low, pltpu.roll(near, LANES - per_half, 1), far)),
            (pltpu.roll(ahead, cells - 1, 1), pltpu.roll(ahead, per_half - 1, 1)),
            (pltpu.roll(behind, LANES - per_half + 1, 1), pltpu.roll(behind, LANES - cells + 1, 1)),
        )
        for which in range(3):
            for look in range(look_count):
                unfolded[3 * k + which, pl.ds(look, row_tiles, stride=look_count), :] = expanded[which][look]
        main = unfolded[3 * k]
        if k < 2:
            dense[k] = main
        after = unfolded[3 * k + 1] * has_right
        before = unfolded[3 * k + 2] * has_left
        right = jnp.where(right_edge, after, pltpu.roll(main, LANES - 1, 1))
        left = jnp.where(left_edge, before, pltpu.roll(main, 1, 1))
        wide = main + left + right
        up = jnp.where(line == 0, 0.0, pltpu.roll(wide, 1, 0))
        down = jnp.where(line == look_rows - 1, 0.0, pltpu.roll(wide, look_rows - 1, 0))
        sums.append(wide + up + down)
    magnitude = jnp.sqrt(sums[0] * sums[0] + sums[1] * sums[1])
    dense[2] = magnitude / (jnp.sqrt(sums[2] * sums[3]) + EPSILON)

    drain(blocks.at[:, :, pl.ds(0, (dates - 1) * TILE)], sems.at[0])
    drain(outbox.at[pl.ds(0, dates - 1)], sems.at[2])
    drain(outbox, sems.at[5])


def spread(slots, dense, ifg, coh):
    cells = ifg.shape[-1]
    for slot in range(slots):
        part = slice(slot * cells, (slot + 1) * cells)
        ifg[0, 0, slot] = dense[0, :, part]
        ifg[1, 0, slot] = dense[1, :, part]
        coh[0, slot] = dense[2, :, part]


def solution(mesh):
    dates, cols = mesh.shape["date"], mesh.shape["col"]

    def shards(slc, offsets):
        rows, columns = slc.shape[2], slc.shape[3]
        slots = offsets.shape[1]
        row_tiles = rows // TILE
        halves = dates // row_tiles
        if halves != 2 or slots * columns // LOOK_COLS != LANES:
            raise ValueError("unsupported sizes")
        width = columns // halves
        look_rows, cells = rows // LOOK_ROWS, columns // LOOK_COLS
        tiles = slc.reshape(2, row_tiles, TILE, columns // LANES, LANES).transpose(0, 1, 3, 2, 4)
        dense = pl.pallas_call(
            functools.partial(kernel, dates, cols, slots),
            out_shape=jax.ShapeDtypeStruct((3, look_rows, LANES), jnp.float32),
            in_specs=[pl.BlockSpec(memory_space=pltpu.HBM)] * 2,
            out_specs=pl.BlockSpec(memory_space=pltpu.VMEM),
            scratch_shapes=[
                pltpu.VMEM((2, width // LANES, dates * TILE, LANES), jnp.float32),
                pltpu.VMEM((slots, dates), jnp.int32),
                pltpu.VMEM((dates, 4, LANES), jnp.float32),
                pltpu.VMEM((halves, row_tiles, 4, LANES), jnp.float32),
                pltpu.VMEM((halves, row_tiles, 4, LANES), jnp.float32),
                pltpu.VMEM((12, look_rows, LANES), jnp.float32),
                pltpu.VMEM(tiles.shape, jnp.float32),
                pltpu.SemaphoreType.DMA((8,)),
            ],
            compiler_params=pltpu.CompilerParams(
                collective_id=0, has_side_effects=True, vmem_limit_bytes=8 * 1024 * 1024
            ),
        )(
            pltpu.with_memory_space_constraint(tiles, pltpu.HBM),
            pltpu.with_memory_space_constraint(offsets.T, pltpu.HBM),
        )
        return tuple(
            pl.pallas_call(
                functools.partial(spread, slots),
                out_shape=(
                    jax.ShapeDtypeStruct((2, 1, slots, look_rows, cells), jnp.float32),
                    jax.ShapeDtypeStruct((1, slots, look_rows, cells), jnp.float32),
                ),
                compiler_params=pltpu.CompilerParams(vmem_limit_bytes=1024 * 1024),
            )(dense)
        )

    return jax.shard_map(
        shards,
        mesh=mesh,
        in_specs=(P(None, "date", None, "col"), P()),
        out_specs=(P(None, "date", None, None, "col"), P("date", None, None, "col")),
        check_vma=False,
    )
```

```python
import functools

import jax
import jax.numpy as jnp
from jax import lax
from jax.experimental import pallas as pl
from jax.experimental.pallas import tpu as pltpu
from jax.sharding import PartitionSpec as P

EPSILON = 1e-06
MAX_OFFSET = 6
LOOK_ROWS = 4
LOOK_COLS = 16
TILE = 8
LANES = 128
MESH = pl.DeviceIdType.MESH


def drain(ref, sem):
    pltpu.make_async_copy(ref, ref, sem).wait()


def split_dot(values, pool):
    total = None
    for _ in range(3):
        part = values.astype(jnp.bfloat16)
        values = values - part.astype(jnp.float32)
        dot = jnp.dot(part, pool, preferred_element_type=jnp.float32)
        total = dot if total is None else total + dot
    return total


def kernel(dates, cols, slots, slc, offsets, dense, blocks, offs, outbox, landed, halo, unfolded, staged, sems):
    date, col = lax.axis_index("date"), lax.axis_index("col")
    chunks = blocks.shape[1]
    width = chunks * LANES
    halves = slc.shape[2] // chunks
    cells = slc.shape[2] * LANES // LOOK_COLS
    rt, half = date // halves, date % halves
    side = lax.rem(col + cols + 2 * half - 1, cols)

    order = sorted(range(1, dates), key=lambda step: abs(2 * step - dates))

    barrier = pltpu.get_barrier_semaphore()
    for step in order:
        peer = lax.rem(date + step, dates)
        pl.semaphore_signal(barrier, inc=1, device_id=(peer, col), device_id_type=MESH)
    for step in (1, cols - 1):
        other = lax.rem(col + step, cols)
        pl.semaphore_signal(barrier, inc=1, device_id=(date, other), device_id_type=MESH)

    offs_copy = pltpu.make_async_copy(offsets, offs, sems.at[4])
    offs_copy.start()

    stage_copy = pltpu.make_async_copy(slc, staged, sems.at[7])
    stage_copy.start()

    def tile_of(source, peer):
        return source.at[:, peer // halves, pl.ds((peer % halves) * chunks, chunks)]

    my_rows = pl.ds(pl.multiple_of(date * TILE, TILE), TILE)
    pltpu.make_async_copy(tile_of(slc, date), blocks.at[:, :, my_rows], sems.at[6]).start()

    pl.semaphore_wait(barrier, dates + 1)
    stage_copy.wait()

    for step in order:
        peer = lax.rem(date + step, dates)
        pltpu.make_async_remote_copy(
            src_ref=tile_of(staged, peer),
            dst_ref=blocks.at[:, :, my_rows],
            send_sem=sems.at[0],
            recv_sem=sems.at[6],
            device_id=(peer, col),
            device_id_type=MESH,
        ).start()

    looked_col = lax.broadcasted_iota(jnp.int32, (width, LANES), 0) // LOOK_COLS
    per_half = width // LOOK_COLS
    shown = lax.broadcasted_iota(jnp.int32, (width, LANES), 1) % per_half
    pool = jnp.where(looked_col == shown, 1.0 / (LOOK_ROWS * LOOK_COLS), 0.0).astype(jnp.bfloat16)
    lane = lax.broadcasted_iota(jnp.int32, (dates, LANES), 1)
    offs_copy.wait()
    lane_off = jnp.zeros((dates, LANES), jnp.int32)
    eye = lax.broadcasted_iota(jnp.int32, (dates, dates), 0) == lax.broadcasted_iota(
        jnp.int32, (dates, dates), 1
    )
    for slot in range(slots):
        row = offs[slot : slot + 1, :].astype(jnp.float32)
        column = jnp.sum(jnp.where(eye, row, 0.0), axis=1, keepdims=True).astype(jnp.int32)
        mine = lane // cells == slot
        lane_off = jnp.where(mine, column, lane_off)
    chosen = [lane_off == o for o in range(1, MAX_OFFSET + 1)]

    look_count = TILE // LOOK_ROWS
    pooled = None
    drain(blocks, sems.at[6])
    for chunk in range(chunks):
        pieces = []
        for look in range(look_count):
            real_sums = [None] * MAX_OFFSET
            imag_sums = [None] * MAX_OFFSET
            power = None
            for row in range(look * LOOK_ROWS, (look + 1) * LOOK_ROWS):
                a0 = blocks[0, chunk, pl.ds(row, dates, stride=TILE), :]
                a1 = blocks[1, chunk, pl.ds(row, dates, stride=TILE), :]
                squares = a0 * a0 + a1 * a1
                power = squares if power is None else power + squares
                for o in range(MAX_OFFSET):
                    b0 = pltpu.roll(a0, dates - 1 - o, 0)
                    b1 = pltpu.roll(a1, dates - 1 - o, 0)
                    real = a0 * b0 + a1 * b1
                    imag = a1 * b0 - a0 * b1
                    real_sums[o] = real if real_sums[o] is None else real_sums[o] + real
                    imag_sums[o] = imag if imag_sums[o] is None else imag_sums[o] + imag
            pieces += real_sums + imag_sums + [power]
        part = split_dot(
            jnp.concatenate(pieces, axis=0), pool[chunk * LANES : (chunk + 1) * LANES]
        )
        pooled = part if pooled is None else pooled + part

    count = 2 * MAX_OFFSET + 1
    first = (lane % cells) // per_half == 0
    part = [
        jnp.where(
            first,
            pooled[q * dates : (q + 1) * dates],
            pooled[(count + q) * dates : (count + q + 1) * dates],
        )
        for q in range(count)
    ]
    planes = [jnp.zeros((dates, LANES), jnp.float32) for _ in range(4)]
    for o in range(1, MAX_OFFSET + 1):
        take = chosen[o - 1]
        planes[0] = jnp.where(take, part[o - 1], planes[0])
        planes[1] = jnp.where(take, part[MAX_OFFSET + o - 1], planes[1])
        planes[2] = jnp.where(take, part[2 * MAX_OFFSET], planes[2])
        planes[3] = jnp.where(take, pltpu.roll(part[2 * MAX_OFFSET], dates - o, 0), planes[3])
    for k in range(4):
        outbox[:, k, :] = planes[k]

    for step in order + [0]:
        peer = lax.rem(date + step, dates)
        tile = outbox.at[peer]
        if step:
            pltpu.make_async_remote_copy(
                src_ref=tile,
                dst_ref=landed.at[half, rt],
                send_sem=sems.at[2],
                recv_sem=sems.at[3],
                device_id=(peer, col),
                device_id_type=MESH,
            ).start()
        else:
            pltpu.make_async_copy(tile, landed.at[half, rt], sems.at[3]).start()
        pltpu.make_async_remote_copy(
            src_ref=tile,
            dst_ref=halo.at[half, rt],
            send_sem=sems.at[5],
            recv_sem=sems.at[1],
            device_id=(peer, side),
            device_id_type=MESH,
        ).start()

    row_tiles = landed.shape[1]
    look_rows = row_tiles * look_count
    lane = lax.broadcasted_iota(jnp.int32, (look_rows, LANES), 1) % cells
    line = lax.broadcasted_iota(jnp.int32, (look_rows, LANES), 0)
    left_edge, right_edge = lane == 0, lane == cells - 1
    has_left = jnp.where(col > 0, 1.0, 0.0)
    has_right = jnp.where(col < cols - 1, 1.0, 0.0)

    drain(landed, sems.at[3])
    drain(halo, sems.at[1])
    sums = []
    for k in range(4):
        ahead, behind = halo[0, :, k, :], halo[1, :, k, :]
        near, far = landed[0, :, k, :], landed[1, :, k, :]
        low = first[0:1]
        expanded = (
            (jnp.where(low, near, pltpu.roll(far, per_half, 1)), jnp.where(low, pltpu.roll(near, LANES - per_half, 1), far)),
            (pltpu.roll(ahead, cells - 1, 1), pltpu.roll(ahead, per_half - 1, 1)),
            (pltpu.roll(behind, LANES - per_half + 1, 1), pltpu.roll(behind, LANES - cells + 1, 1)),
        )
        for which in range(3):
            for look in range(look_count):
                unfolded[3 * k + which, pl.ds(look, row_tiles, stride=look_count), :] = expanded[which][look]
        main = unfolded[3 * k]
        if k < 2:
            dense[k] = main
        after = unfolded[3 * k + 1] * has_right
        before = unfolded[3 * k + 2] * has_left
        right = jnp.where(right_edge, after, pltpu.roll(main, LANES - 1, 1))
        left = jnp.where(left_edge, before, pltpu.roll(main, 1, 1))
        wide = main + left + right
        up = jnp.where(line == 0, 0.0, pltpu.roll(wide, 1, 0))
        down = jnp.where(line == look_rows - 1, 0.0, pltpu.roll(wide, look_rows - 1, 0))
        sums.append(wide + up + down)
    magnitude = jnp.sqrt(sums[0] * sums[0] + sums[1] * sums[1])
    dense[2] = magnitude / (jnp.sqrt(sums[2] * sums[3]) + EPSILON)

    drain(blocks.at[:, :, pl.ds(0, (dates - 1) * TILE)], sems.at[0])
    drain(outbox.at[pl.ds(0, dates - 1)], sems.at[2])
    drain(outbox, sems.at[5])


def spread(slots, dense, ifg, coh):
    cells = ifg.shape[-1]
    for slot in range(slots):
        part = slice(slot * cells, (slot + 1) * cells)
        ifg[0, 0, slot] = dense[0, :, part]
        ifg[1, 0, slot] = dense[1, :, part]
        coh[0, slot] = dense[2, :, part]


def solution(mesh):
    dates, cols = mesh.shape["date"], mesh.shape["col"]

    def shards(slc, offsets):
        rows, columns = slc.shape[2], slc.shape[3]
        slots = offsets.shape[1]
        row_tiles = rows // TILE
        halves = dates // row_tiles
        if halves != 2 or slots * columns // LOOK_COLS != LANES:
            raise ValueError("unsupported sizes")
        width = columns // halves
        look_rows, cells = rows // LOOK_ROWS, columns // LOOK_COLS
        tiles = slc.reshape(2, row_tiles, TILE, columns // LANES, LANES).transpose(0, 1, 3, 2, 4)
        dense = pl.pallas_call(
            functools.partial(kernel, dates, cols, slots),
            out_shape=jax.ShapeDtypeStruct((3, look_rows, LANES), jnp.float32),
            in_specs=[pl.BlockSpec(memory_space=pltpu.HBM)] * 2,
            out_specs=pl.BlockSpec(memory_space=pltpu.VMEM),
            scratch_shapes=[
                pltpu.VMEM((2, width // LANES, dates * TILE, LANES), jnp.float32),
                pltpu.VMEM((slots, dates), jnp.int32),
                pltpu.VMEM((dates, 4, LANES), jnp.float32),
                pltpu.VMEM((halves, row_tiles, 4, LANES), jnp.float32),
                pltpu.VMEM((halves, row_tiles, 4, LANES), jnp.float32),
                pltpu.VMEM((12, look_rows, LANES), jnp.float32),
                pltpu.VMEM(tiles.shape, jnp.float32),
                pltpu.SemaphoreType.DMA((8,)),
            ],
            compiler_params=pltpu.CompilerParams(
                collective_id=0, has_side_effects=True, vmem_limit_bytes=8 * 1024 * 1024
            ),
        )(
            pltpu.with_memory_space_constraint(tiles, pltpu.HBM),
            pltpu.with_memory_space_constraint(offsets.T, pltpu.HBM),
        )
        return tuple(
            pl.pallas_call(
                functools.partial(spread, slots),
                out_shape=(
                    jax.ShapeDtypeStruct((2, 1, slots, look_rows, cells), jnp.float32),
                    jax.ShapeDtypeStruct((1, slots, look_rows, cells), jnp.float32),
                ),
                compiler_params=pltpu.CompilerParams(vmem_limit_bytes=1024 * 1024),
            )(dense)
        )

    return jax.shard_map(
        shards,
        mesh=mesh,
        in_specs=(P(None, "date", None, "col"), P()),
        out_specs=(P(None, "date", None, None, "col"), P("date", None, None, "col")),
        check_vma=False,
    )
```
